512 devices in a mesh: src: 16 (over z_lo, core), rcv: 32 (over y, x, z_hi).
Axes of the slice: x: 4, y: 4, z: 16 (z_hi: 2, z_lo: 8; z = z_hi * 8 + z_lo), core: 2. Of those that a mesh axis runs over, the one named last changes fastest.
Arguments:
- spectra: bfloat16 [768, 2, 2, 10240], P('rcv', None, None, 'src'), may hold values from -4000 to 4000
Outputs:
- cross: float32 [10240, 2, 2, 10240], P('src', None, None, 'rcv')
The draws below stay inside these ranges and needn't reach their ends.
All inputs are finite; a program needn't handle non-finite values.
Results may differ from the reference program's by a relative error of at most 0.0037.
Values may be sent and summed in bfloat16 or wider, within the bound.
No kernel may reach another device: no remote copies, remote signals or barrier semaphores. Data moves between devices by JAX's collectives and lax.ppermute only.
A program may use at most 64 MiB of HBM per device.

```python
import math
import jax
import jax.numpy as jnp
from jax import lax

CHANNELS = 10240
FREQS = 2
WINDOWS = 768
N_SRC = 16


def draw_spectra(key, part):
    key = jax.random.fold_in(key, 11)
    keys = jax.random.split(key, 4)
    shape = (WINDOWS, 2, FREQS, CHANNELS)
    window_index = jnp.arange(WINDOWS, dtype=jnp.float32)
    jitter = jnp.clip(jax.random.normal(keys[0], (WINDOWS,), jnp.float32), -3.0, 3.0)
    ramp = 10.0 ** (window_index / max(WINDOWS - 1, 1)) * jnp.exp(0.25 * jitter)
    freq_gain = jnp.exp(jax.random.uniform(keys[1], (FREQS,), jnp.float32, math.log(0.5), math.log(2.0)))
    chan_gain = jnp.exp(jax.random.uniform(keys[2], (CHANNELS,), jnp.float32, 0.0, math.log(10.0)))
    base = jnp.clip(jax.random.normal(keys[3], shape, jnp.float32), -5.0, 5.0)
    values = base * ramp[:, None, None, None] * freq_gain[None, None, :, None] * chan_gain[None, None, None, :]
    return values.astype(jnp.bfloat16)


def setup_inputs(seed: int = 0) -> dict:
    key_of = jax.random.split(jax.random.key(seed), 2)
    spectra = draw_spectra(jax.random.fold_in(key_of[1], 71), 0)
    return {"spectra": spectra}


water_factor = 0.5
tiny_eps = 1e-06

def whiten_all(spectra):
    values = spectra.astype(jnp.float32)
    energy = values[:, 0] ** 2 + values[:, 1] ** 2
    water_level = lax.optimization_barrier(jnp.mean(energy, axis=0))
    denom = jnp.sqrt(energy + water_factor * water_level[None] + tiny_eps)
    return (values / denom[:, None]).astype(jnp.bfloat16)

def reference(spectra):
    whitened = whiten_all(spectra).astype(jnp.float32)
    flipped = jnp.stack([whitened[:, 1], -whitened[:, 0]], axis=1)
    block_width = CHANNELS // N_SRC
    stack_scale = jnp.float32(1.0 / WINDOWS ** 0.5)

    def source_block(first_row):
        rows_now = lax.dynamic_slice_in_dim(whitened, first_row, block_width, 3)
        flip_now = lax.dynamic_slice_in_dim(flipped, first_row, block_width, 3)
        real_part = jnp.einsum('wpfc,wpfd->cfd', rows_now, whitened)
        imag_part = jnp.einsum('wpfc,wpfd->cfd', flip_now, whitened)
        return jnp.stack([real_part, imag_part], axis=1) * stack_scale
    starts = (jnp.arange(N_SRC) * block_width).astype(jnp.int32)
    blocks = lax.map(source_block, starts)
    return blocks.reshape(CHANNELS, 2, FREQS, CHANNELS)
```

```python
import functools
import math

import jax
import jax.numpy as jnp
from jax import lax
from jax.experimental import pallas as pl
from jax.experimental.pallas import tpu as pltpu
from jax.sharding import Mesh, PartitionSpec as P

water_factor = 0.5
tiny_eps = 1e-06

SIZES = dict(zl=8, core=2, y=4, x=4, zh=2)
AXES = tuple(SIZES)


def coordinates():
    out = [()]
    for size in SIZES.values():
        out = [c + (i,) for c in out for i in range(size)]
    return out


def number(c):
    n = 0
    for i, size in zip(c, SIZES.values()):
        n = n * size + i % size
    return n


def permute(value, target):
    pairs = [(number(c), number(target(*c))) for c in coordinates()]
    return lax.ppermute(value, AXES, pairs)


def fetch_first(value, offset):
    def target(zl, core, y, x, zh):
        return (zl, core, y, x - offset, zh) if core == 0 else (zl, core, y - offset, x, zh)

    return permute(value, target)


def fetch_second(value, offset):
    def target(zl, core, y, x, zh):
        return (zl, core, y - offset, x, zh) if core == 0 else (zl, core, y, x - offset, zh)

    return permute(value, target)


def gather_plane(block):
    first = jnp.stack([block] + [fetch_first(block, o) for o in (1, 2, 3)])
    return [first] + [fetch_second(first, o) for o in (1, 2, 3)]


def to_column(value, cross):
    def target(zl, core, y, x, zh):
        s, g = zl * 2 + core, y * 4 + x
        return (g // 2, g % 2, s // 4, s % 4, 1 - zh if cross else zh)

    return permute(value, target)


def along_column(value, distance):
    return permute(value, lambda zl, core, y, x, zh: (zl ^ distance, core, y, x, zh))


def spectra_kernel(place, *refs):
    sources, receivers, out, wide, left, left_turned = refs[:8], refs[8:10], refs[10], refs[11], refs[12], refs[13]
    zl, core, y, x = place[0], place[1], place[2], place[3]
    rows = sources[0].shape[2]
    half = rows // 2
    channels = sources[0].shape[3]
    width = channels // 2
    windows = 32 * half

    def energy_of(block):
        values = block.astype(jnp.float32)
        real, imag = values[:half], values[half:]
        return real, imag, real * real + imag * imag

    def fold(energy):
        return energy.reshape(half // 8, 8, channels).sum(axis=0)

    def level(total):
        return (water_factor / windows) * jnp.sum(total, axis=0, keepdims=True) + tiny_eps

    zero = jnp.zeros((8, channels), jnp.float32)
    for f in range(2):
        total = zero
        for ref in sources:
            total = lax.fori_loop(0, 4, lambda a, t, ref=ref: t + fold(energy_of(ref[a, f])[2]), total)
        floor = level(total)
        for n, ref in enumerate(sources):
            zr, second = n // 4, n % 4

            def body(a, carry, ref=ref, zr=zr, second=second):
                real, imag, energy = energy_of(ref[a, f])
                scale = lax.rsqrt(energy + floor)
                gy = lax.rem(y + jnp.where(core == 0, second, a), 4)
                gx = lax.rem(x + jnp.where(core == 0, a, second), 4)
                row = pl.multiple_of((zr * 16 + gy * 4 + gx) * rows, rows)
                block = jnp.concatenate([real * scale, imag * scale], axis=0).astype(jnp.bfloat16)
                wide[f, pl.ds(row, rows), :] = block
                return carry

            lax.fori_loop(0, 4, body, 0)

    total = zero
    for ref in receivers:
        total = lax.fori_loop(
            0, 8, lambda a, t, ref=ref: t + fold(energy_of(ref[a, 0])[2]) + fold(energy_of(ref[a, 1])[2]), total
        )
    floor = level(total)
    for n, ref in enumerate(receivers):

        def body(a, carry, ref=ref, n=n):
            other = lax.bitwise_xor(zl, (a % 2) * 4 + (a // 2 % 2) * 2 + a // 4)
            g = other * 2 + lax.bitwise_xor(core, n)
            for zr in range(2):
                real, imag, energy = energy_of(ref[a, zr])
                scale = lax.rsqrt(energy + floor)
                real, imag = real * scale, imag * scale
                row = pl.multiple_of((zr * 16 + g) * rows, rows)
                block = jnp.concatenate([real, imag], axis=0).astype(jnp.bfloat16)
                turned = jnp.concatenate([-imag, real], axis=0).astype(jnp.bfloat16)
                for f in range(2):
                    left[f, pl.ds(row, rows), :] = block[:, f * width : (f + 1) * width]
                    left_turned[f, pl.ds(row, rows), :] = turned[:, f * width : (f + 1) * width]
            return carry

        lax.fori_loop(0, 8, body, 0)

    stack_scale = 1.0 / math.sqrt(windows)
    for f in range(2):
        for part, ref in enumerate((left, left_turned)):
            product = lax.dot_general(
                ref[f], wide[f], (((0,), (0,)), ((), ())), preferred_element_type=jnp.float32
            )
            out[part, f] = product * stack_scale


def cross_spectra(place, sources, receivers):
    depth = 32 * sources[0].shape[2]
    channels = sources[0].shape[3]
    vmem = pl.BlockSpec(memory_space=pltpu.VMEM)
    return pl.pallas_call(
        spectra_kernel,
        out_shape=jax.ShapeDtypeStruct((2, 2, channels // 2, channels), jnp.float32),
        in_specs=[pl.BlockSpec(memory_space=pltpu.SMEM)] + [vmem] * 10,
        out_specs=vmem,
        scratch_shapes=[
            pltpu.VMEM((2, depth, channels), jnp.bfloat16),
            pltpu.VMEM((2, depth, channels // 2), jnp.bfloat16),
            pltpu.VMEM((2, depth, channels // 2), jnp.bfloat16),
        ],
        compiler_params=pltpu.CompilerParams(vmem_limit_bytes=48 * 1024 * 1024),
    )(place, *sources, *receivers)


def on_device(spectra):
    windows, _, freqs, channels = spectra.shape
    width = channels // 2
    place = jnp.stack([lax.axis_index(a) for a in ("zl", "core", "y", "x")]).astype(jnp.int32)
    zh = lax.axis_index("zh")
    block = jnp.transpose(spectra, (2, 1, 0, 3)).reshape(freqs, 2 * windows, channels)

    low = jnp.concatenate([block[0, :, :width], block[1, :, :width]], axis=1)
    high = jnp.concatenate([block[0, :, width:], block[1, :, width:]], axis=1)
    mine = jnp.where(zh == 0, low, high)
    theirs = jnp.where(zh == 0, high, low)
    held = jnp.stack([to_column(mine, False), to_column(theirs, True)])[None]
    partner = permute(block, lambda zl, core, y, x, zh: (zl, core, y, x, 1 - zh))
    sources = gather_plane(block) + gather_plane(partner)

    for distance in (4, 2, 1):
        held = jnp.concatenate([held, along_column(held, distance)])
    other = permute(held, lambda zl, core, y, x, zh: (zl, 1 - core, y, x, zh))

    crossed = cross_spectra(place, sources, [held, other])
    return jnp.transpose(crossed, (3, 0, 1, 2))


def solution(mesh):
    fine = Mesh(mesh.devices.reshape(tuple(SIZES.values())), AXES)
    return jax.shard_map(
        on_device,
        mesh=fine,
        in_specs=(P(("y", "x", "zh"), None, None, ("zl", "core")),),
        out_specs=P(("zl", "core"), None, None, ("y", "x", "zh")),
        check_vma=False,
    )
```

```python
import functools
import math

import jax
import jax.numpy as jnp
from jax import lax
from jax.experimental import pallas as pl
from jax.experimental.pallas import tpu as pltpu
from jax.sharding import Mesh, PartitionSpec as P

water_factor = 0.5
tiny_eps = 1e-06

SIZES = dict(zl=8, core=2, y=4, x=4, zh=2)
AXES = tuple(SIZES)


def coordinates():
    out = [()]
    for size in SIZES.values():
        out = [c + (i,) for c in out for i in range(size)]
    return out


def number(c):
    n = 0
    for i, size in zip(c, SIZES.values()):
        n = n * size + i % size
    return n


def permute(value, target):
    pairs = [(number(c), number(target(*c))) for c in coordinates()]
    return lax.ppermute(value, AXES, pairs)


def fetch_first(value, offset):
    def target(zl, core, y, x, zh):
        return (zl, core, y, x - offset, zh) if core == 0 else (zl, core, y - offset, x, zh)

    return permute(value, target)


def fetch_second(value, offset):
    def target(zl, core, y, x, zh):
        return (zl, core, y - offset, x, zh) if core == 0 else (zl, core, y, x - offset, zh)

    return permute(value, target)


def gather_first(blocks):
    return jnp.stack([blocks] + [fetch_first(blocks, o) for o in (1, 2, 3)])


def gather_second(first):
    return [first] + [fetch_second(first, o) for o in (1, 2, 3)]


def to_column(value, cross):
    def target(zl, core, y, x, zh):
        s, g = zl * 2 + core, y * 4 + x
        return (g // 2, g % 2, s // 4, s % 4, 1 - zh if cross else zh)

    return permute(value, target)


def along_column(value, distance):
    return permute(value, lambda zl, core, y, x, zh: (zl ^ distance, core, y, x, zh))


def energy_of(block):
    values = block.astype(jnp.float32)
    half = values.shape[0] // 2
    real, imag = values[:half], values[half:]
    return real, imag, real * real + imag * imag


def fold(energy):
    return energy.reshape(energy.shape[0] // 8, 8, energy.shape[1]).sum(axis=0)


def floor_of(total, windows):
    return (water_factor / windows) * jnp.sum(total, axis=0, keepdims=True) + tiny_eps


def stacked(upper, lower):
    return jnp.concatenate([upper, lower], axis=0).astype(jnp.bfloat16)


def whiten_kernel(place, *refs):
    sources, wide = refs[:4], refs[4]
    core, y, x = place[1], place[2], place[3]
    freqs, rows, channels = sources[0].shape[2:]
    windows = 16 * rows
    for f in range(freqs):

        def add(a, total):
            for ref in sources:
                for zr in range(2):
                    total = total + fold(energy_of(ref[a, zr, f])[2])
            return total

        floor = floor_of(lax.fori_loop(0, 4, add, jnp.zeros((8, channels), jnp.float32)), windows)

        def whiten(a, carry):
            for second, ref in enumerate(sources):
                gy = lax.rem(y + jnp.where(core == 0, second, a), 4)
                gx = lax.rem(x + jnp.where(core == 0, a, second), 4)
                for zr in range(2):
                    real, imag, energy = energy_of(ref[a, zr, f])
                    scale = lax.rsqrt(energy + floor)
                    real, imag = real * scale, imag * scale
                    row = pl.multiple_of((zr * 16 + gy * 4 + gx) * rows, rows)
                    wide[f, pl.ds(row, rows), :channels] = stacked(real, imag)
                    wide[f, pl.ds(row, rows), channels:] = stacked(imag, -real)
            return carry

        lax.fori_loop(0, 4, whiten, 0)


def multiply_kernel(place, held, other, wide, arrived, out, left):
    del arrived
    zl, core = place[0], place[1]
    rows, channels = held.shape[2:]
    width = channels // 2
    windows = 16 * rows

    def add(a, total):
        for ref in (held, other):
            for zr in range(2):
                total = total + fold(energy_of(ref[a, zr])[2])
        return total

    floor = floor_of(lax.fori_loop(0, 8, add, jnp.zeros((8, channels), jnp.float32)), windows)

    def whiten(a, carry):
        along = lax.bitwise_xor(zl, (a % 2) * 4 + (a // 2 % 2) * 2 + a // 4)
        for n, ref in enumerate((held, other)):
            g = along * 2 + lax.bitwise_xor(core, n)
            for zr in range(2):
                real, imag, energy = energy_of(ref[a, zr])
                scale = lax.rsqrt(energy + floor)
                row = pl.multiple_of((zr * 16 + g) * rows, rows)
                block = stacked(real * scale, imag * scale)
                for f in range(2):
                    left[f, pl.ds(row, rows), :] = block[:, f * width : (f + 1) * width]
        return carry

    lax.fori_loop(0, 8, whiten, 0)
    stack_scale = 1.0 / math.sqrt(windows)
    for f in range(2):
        product = lax.dot_general(left[f], wide[f], (((0,), (0,)), ((), ())), preferred_element_type=jnp.float32)
        product = product * stack_scale
        out[0, f] = product[:, :channels]
        out[1, f] = product[:, channels:]


VMEM = pl.BlockSpec(memory_space=pltpu.VMEM)
SMEM = pl.BlockSpec(memory_space=pltpu.SMEM)


def whiten_sources(place, sources):
    freqs, rows, channels = sources[0].shape[2:]
    depth = 32 * rows
    return pl.pallas_call(
        whiten_kernel,
        out_shape=jax.ShapeDtypeStruct((freqs, depth, 2 * channels), jnp.bfloat16),
        in_specs=[SMEM] + [VMEM] * 4,
        out_specs=VMEM,
        compiler_params=pltpu.CompilerParams(vmem_limit_bytes=20 * 1024 * 1024),
        cost_estimate=pl.CostEstimate(flops=20 * depth * channels, bytes_accessed=8 * depth * channels, transcendentals=depth * channels),
    )(place, *sources)


def multiply(place, held, other, wide, arrived):
    rows, channels = held.shape[2:]
    depth = 32 * rows
    return pl.pallas_call(
        multiply_kernel,
        out_shape=jax.ShapeDtypeStruct((2, 2, channels // 2, channels), jnp.float32),
        in_specs=[SMEM] + [VMEM] * 4,
        out_specs=VMEM,
        scratch_shapes=[pltpu.VMEM((2, depth, channels // 2), jnp.bfloat16)],
        compiler_params=pltpu.CompilerParams(vmem_limit_bytes=20 * 1024 * 1024),
    )(place, held, other, wide, arrived)


def on_device(spectra):
    windows, _, freqs, channels = spectra.shape
    width = channels // 2
    place = jnp.stack([lax.axis_index(a) for a in ("zl", "core", "y", "x")]).astype(jnp.int32)
    zh = lax.axis_index("zh")
    block = jnp.transpose(spectra, (2, 1, 0, 3)).reshape(freqs, 2 * windows, channels)

    low = jnp.concatenate([block[0, :, :width], block[1, :, :width]], axis=1)
    high = jnp.concatenate([block[0, :, width:], block[1, :, width:]], axis=1)
    mine = jnp.where(zh == 0, low, high)
    theirs = jnp.where(zh == 0, high, low)
    held = jnp.stack([to_column(mine, False), to_column(theirs, True)])[None]
    partner = permute(block, lambda zl, core, y, x, zh: (zl, core, y, x, 1 - zh))
    held, partner = lax.optimization_barrier((held, partner))
    first = gather_first(jnp.stack([block, partner]))
    held = jnp.concatenate([held, along_column(held, 4)])
    held, first = lax.optimization_barrier((held, first))
    sources = gather_second(first)
    for distance in (2, 1):
        held = jnp.concatenate([held, along_column(held, distance)])
    arrived = jnp.stack([r[0, 0, 0, :16, :128] for r in sources[1:]])
    held, arrived = lax.optimization_barrier((held, arrived))
    wide = whiten_sources(place, sources)
    other = permute(held, lambda zl, core, y, x, zh: (zl, 1 - core, y, x, zh))

    crossed = multiply(place, held, other, wide, arrived)
    return jnp.transpose(crossed, (3, 0, 1, 2))


def solution(mesh):
    fine = Mesh(mesh.devices.reshape(tuple(SIZES.values())), AXES)
    return jax.shard_map(
        on_device,
        mesh=fine,
        in_specs=(P(("y", "x", "zh"), None, None, ("zl", "core")),),
        out_specs=P(("zl", "core"), None, None, ("y", "x", "zh")),
        check_vma=False,
    )
```

```python
import functools
import math

import jax
import jax.numpy as jnp
from jax import lax
from jax.experimental import pallas as pl
from jax.experimental.pallas import tpu as pltpu
from jax.sharding import Mesh, PartitionSpec as P

water_factor = 0.5
tiny_eps = 1e-06

SIZES = dict(zl=8, core=2, y=4, x=4, zh=2)
AXES = tuple(SIZES)


def coordinates():
    out = [()]
    for size in SIZES.values():
        out = [c + (i,) for c in out for i in range(size)]
    return out


def number(c):
    n = 0
    for i, size in zip(c, SIZES.values()):
        n = n * size + i % size
    return n


def permute(value, target):
    pairs = [(number(c), number(target(*c))) for c in coordinates()]
    return lax.ppermute(value, AXES, pairs)


def groups_of(swapped):
    along_x = [[[c * 16 + y * 4 + x for x in range(4)] for y in range(4)] for c in range(2)]
    along_y = [[[c * 16 + y * 4 + x for y in range(4)] for x in range(4)] for c in range(2)]
    return along_y[0] + along_x[1] if swapped else along_x[0] + along_y[1]


def gather_four(value, swapped):
    copies = jnp.broadcast_to(value, (4,) + value.shape)
    return lax.all_to_all(copies, ("core", "y", "x"), 0, 0, axis_index_groups=groups_of(swapped))


def to_column(value, copy, cross):
    def target(zl, core, y, x, zh):
        s, g = zl * 2 + core, y * 4 + x
        group, slot = (g + copy) % 2, g // 2
        return (group * 4 + slot // 2, slot % 2, s // 4, s % 4, 1 - zh if cross else zh)

    return permute(value, target)


def along_column(value, distance):
    return permute(value, lambda zl, core, y, x, zh: (zl ^ distance, core, y, x, zh))


def energy_of(block):
    values = block.astype(jnp.float32)
    half = values.shape[0] // 2
    real, imag = values[:half], values[half:]
    return real, imag, real * real + imag * imag


def fold(energy):
    return energy.reshape(energy.shape[0] // 8, 8, energy.shape[1]).sum(axis=0)


def floor_of(total, windows):
    return (water_factor / windows) * jnp.sum(total, axis=0, keepdims=True) + tiny_eps


def stacked(upper, lower):
    return jnp.concatenate([upper, lower], axis=0).astype(jnp.bfloat16)


def whiten_kernel(place, *refs):
    sources, wide = refs
    core = place[1]
    freqs, rows, channels = sources.shape[3:]
    windows = 16 * rows
    for f in range(freqs):

        def add(second, total):
            for first in range(4):
                for zr in range(2):
                    total = total + fold(energy_of(sources[second, first, zr, f])[2])
            return total

        floor = floor_of(lax.fori_loop(0, 4, add, jnp.zeros((8, channels), jnp.float32)), windows)

        def whiten(second, carry):
            for first in range(4):
                g = jnp.where(core == 0, second * 4 + first, first * 4 + second)
                for zr in range(2):
                    real, imag, energy = energy_of(sources[second, first, zr, f])
                    scale = lax.rsqrt(energy + floor)
                    real, imag = real * scale, imag * scale
                    row = pl.multiple_of((zr * 16 + g) * rows, rows)
                    wide[f, pl.ds(row, rows), :channels] = stacked(real, imag)
                    wide[f, pl.ds(row, rows), channels:] = stacked(imag, -real)
            return carry

        lax.fori_loop(0, 4, whiten, 0)


def multiply_kernel(place, held, other, wide, out, left):
    zl, core = place[0], place[1]
    rows, channels = held.shape[2:]
    width = channels // 2
    windows = 16 * rows

    @pl.when(pl.program_id(0) == 0)
    def _():
        def add(a, total):
            for ref in (held, other):
                for zr in range(2):
                    total = total + fold(energy_of(ref[a, zr])[2])
            return total

        floor = floor_of(lax.fori_loop(0, 8, add, jnp.zeros((8, channels), jnp.float32)), windows)

        def whiten(a, carry):
            along = lax.rem(lax.bitwise_xor(zl, a // 2), 4)
            copy = lax.rem(zl // 4 + a, 2)
            for n, ref in enumerate((held, other)):
                g = along * 4 + lax.bitwise_xor(core, n) * 2 + copy
                for zr in range(2):
                    real, imag, energy = energy_of(ref[a, zr])
                    scale = lax.rsqrt(energy + floor)
                    row = pl.multiple_of((zr * 16 + g) * rows, rows)
                    block = stacked(real * scale, imag * scale)
                    for f in range(2):
                        left[f, pl.ds(row, rows), :] = block[:, f * width : (f + 1) * width]
            return carry

        lax.fori_loop(0, 8, whiten, 0)

    stack_scale = 1.0 / math.sqrt(windows)
    product = lax.dot_general(
        left[pl.program_id(0)], wide[0], (((0,), (0,)), ((), ())), preferred_element_type=jnp.float32
    )
    product = product * stack_scale
    out[0, 0] = product[:, :channels]
    out[1, 0] = product[:, channels:]


VMEM = pl.BlockSpec(memory_space=pltpu.VMEM)
SMEM = pl.BlockSpec(memory_space=pltpu.SMEM)


def whiten_sources(place, sources):
    freqs, rows, channels = sources.shape[3:]
    depth = 32 * rows
    return pl.pallas_call(
        whiten_kernel,
        out_shape=jax.ShapeDtypeStruct((freqs, depth, 2 * channels), jnp.bfloat16),
        in_specs=[SMEM, VMEM],
        out_specs=VMEM,
        compiler_params=pltpu.CompilerParams(vmem_limit_bytes=20 * 1024 * 1024),
    )(place, sources)


def multiply(place, held, other, wide):
    rows, channels = held.shape[2:]
    depth, width = 32 * rows, channels // 2
    return pl.pallas_call(
        multiply_kernel,
        grid=(2,),
        out_shape=jax.ShapeDtypeStruct((2, 2, width, channels), jnp.float32),
        in_specs=[SMEM, VMEM, VMEM, pl.BlockSpec((1, depth, 2 * channels), lambda f: (f, 0, 0))],
        out_specs=pl.BlockSpec((2, 1, width, channels), lambda f: (0, f, 0, 0)),
        scratch_shapes=[pltpu.VMEM((2, depth, width), jnp.bfloat16)],
        compiler_params=pltpu.CompilerParams(vmem_limit_bytes=28 * 1024 * 1024),
    )(place, held, other, wide)


def on_device(spectra):
    windows, _, freqs, channels = spectra.shape
    width = channels // 2
    place = jnp.stack([lax.axis_index(a) for a in ("zl", "core", "y", "x")]).astype(jnp.int32)
    zh = lax.axis_index("zh")
    block = jnp.transpose(spectra, (2, 1, 0, 3)).reshape(freqs, 2 * windows, channels)

    def half_of(b):
        low = jnp.concatenate([b[0, :, :width], b[1, :, :width]], axis=1)
        high = jnp.concatenate([b[0, :, width:], b[1, :, width:]], axis=1)
        return jnp.where(zh == 0, low, high)

    partner = permute(block, lambda zl, core, y, x, zh: (zl, core, y, x, 1 - zh))
    pieces = jnp.stack([half_of(block), half_of(partner)])
    first = gather_four(jnp.stack([block, partner]), False)
    held = jnp.stack([to_column(pieces, c, False) for c in range(2)])
    held, first = lax.optimization_barrier((held, first))
    wide = whiten_sources(place, gather_four(first, True))
    held = jnp.concatenate([held] + [along_column(held, d) for d in (1, 2, 3)])
    other = permute(held, lambda zl, core, y, x, zh: (zl, 1 - core, y, x, zh))

    crossed = multiply(place, held, other, wide)
    return jnp.transpose(crossed, (3, 0, 1, 2))


def solution(mesh):
    fine = Mesh(mesh.devices.reshape(tuple(SIZES.values())), AXES)
    return jax.shard_map(
        on_device,
        mesh=fine,
        in_specs=(P(("y", "x", "zh"), None, None, ("zl", "core")),),
        out_specs=P(("zl", "core"), None, None, ("y", "x", "zh")),
        check_vma=False,
    )
```

```python
import functools
import math

import jax
import jax.numpy as jnp
from jax import lax
from jax.experimental import pallas as pl
from jax.experimental.pallas import tpu as pltpu
from jax.sharding import Mesh, PartitionSpec as P

water_factor = 0.5
tiny_eps = 1e-06

SIZES = dict(zl=8, core=2, y=4, x=4, zh=2)
AXES = tuple(SIZES)


def coordinates():
    out = [()]
    for size in SIZES.values():
        out = [c + (i,) for c in out for i in range(size)]
    return out


def number(c):
    n = 0
    for i, size in zip(c, SIZES.values()):
        n = n * size + i % size
    return n


def permute(value, target):
    pairs = [(number(c), number(target(*c))) for c in coordinates()]
    return lax.ppermute(value, AXES, pairs)


def gather_plane(block):
    copies = jnp.broadcast_to(block, (16,) + block.shape)
    return lax.all_to_all(copies, ("y", "x"), 0, 0)


def to_column(value, copy, cross):
    def target(zl, core, y, x, zh):
        s, g = zl * 2 + core, y * 4 + x
        group, slot = (g + copy) % 2, g // 2
        return (group * 4 + slot // 2, slot % 2, s // 4, s % 4, 1 - zh if cross else zh)

    return permute(value, target)


def along_column(value, distance):
    return permute(value, lambda zl, core, y, x, zh: (zl ^ distance, core, y, x, zh))


def energy_of(block):
    values = block.astype(jnp.float32)
    half = values.shape[0] // 2
    real, imag = values[:half], values[half:]
    return real, imag, real * real + imag * imag


def fold(energy):
    return energy.reshape(energy.shape[0] // 8, 8, energy.shape[1]).sum(axis=0)


def floor_of(total, windows):
    return (water_factor / windows) * jnp.sum(total, axis=0, keepdims=True) + tiny_eps


def stacked(upper, lower):
    return jnp.concatenate([upper, lower], axis=0).astype(jnp.bfloat16)


def whiten_kernel(place, *refs):
    sources, wide = refs[:2], refs[2]
    freqs, rows, channels = sources[0].shape[1:]
    windows = 16 * rows
    for f in range(freqs):

        def add(a, total):
            for i in range(4):
                for ref in sources:
                    total = total + fold(energy_of(ref[a * 4 + i, f])[2])
            return total

        floor = floor_of(lax.fori_loop(0, 4, add, jnp.zeros((8, channels), jnp.float32)), windows)

        def whiten(a, carry):
            for i in range(4):
                for zr, ref in enumerate(sources):
                    real, imag, energy = energy_of(ref[a * 4 + i, f])
                    scale = lax.rsqrt(energy + floor)
                    real, imag = real * scale, imag * scale
                    row = pl.multiple_of((zr * 16 + a * 4 + i) * rows, rows)
                    wide[f, pl.ds(row, rows), :channels] = stacked(real, imag)
                    wide[f, pl.ds(row, rows), channels:] = stacked(imag, -real)
            return carry

        lax.fori_loop(0, 4, whiten, 0)


def multiply_kernel(place, held, other, wide, out, left):
    zl, core = place[0], place[1]
    rows, channels = held.shape[2:]
    width = channels // 2
    windows = 16 * rows

    @pl.when(pl.program_id(0) == 0)
    def _():
        def add(a, total):
            for ref in (held, other):
                for zr in range(2):
                    total = total + fold(energy_of(ref[a, zr])[2])
            return total

        floor = floor_of(lax.fori_loop(0, 8, add, jnp.zeros((8, channels), jnp.float32)), windows)

        def whiten(a, carry):
            along = lax.rem(lax.bitwise_xor(zl, a // 2), 4)
            copy = lax.rem(zl // 4 + a, 2)
            for n, ref in enumerate((held, other)):
                g = along * 4 + lax.bitwise_xor(core, n) * 2 + copy
                for zr in range(2):
                    real, imag, energy = energy_of(ref[a, zr])
                    scale = lax.rsqrt(energy + floor)
                    row = pl.multiple_of((zr * 16 + g) * rows, rows)
                    block = stacked(real * scale, imag * scale)
                    for f in range(2):
                        left[f, pl.ds(row, rows), :] = block[:, f * width : (f + 1) * width]
            return carry

        lax.fori_loop(0, 8, whiten, 0)

    stack_scale = 1.0 / math.sqrt(windows)
    product = lax.dot_general(
        left[pl.program_id(0)], wide[0], (((0,), (0,)), ((), ())), preferred_element_type=jnp.float32
    )
    product = product * stack_scale
    out[0, 0] = product[:, :channels]
    out[1, 0] = product[:, channels:]


VMEM = pl.BlockSpec(memory_space=pltpu.VMEM)
SMEM = pl.BlockSpec(memory_space=pltpu.SMEM)


def whiten_sources(place, sources):
    freqs, rows, channels = sources[0].shape[1:]
    depth = 32 * rows
    return pl.pallas_call(
        whiten_kernel,
        out_shape=jax.ShapeDtypeStruct((freqs, depth, 2 * channels), jnp.bfloat16),
        in_specs=[SMEM] + [VMEM] * 2,
        out_specs=VMEM,
        compiler_params=pltpu.CompilerParams(vmem_limit_bytes=20 * 1024 * 1024),
        cost_estimate=pl.CostEstimate(flops=20 * depth * channels, bytes_accessed=8 * depth * channels, transcendentals=depth * channels),
    )(place, *sources)


def multiply(place, held, other, wide):
    rows, channels = held.shape[2:]
    depth, width = 32 * rows, channels // 2
    return pl.pallas_call(
        multiply_kernel,
        grid=(2,),
        out_shape=jax.ShapeDtypeStruct((2, 2, width, channels), jnp.float32),
        in_specs=[SMEM, VMEM, VMEM, pl.BlockSpec((1, depth, 2 * channels), lambda f: (f, 0, 0))],
        out_specs=pl.BlockSpec((2, 1, width, channels), lambda f: (0, f, 0, 0)),
        scratch_shapes=[pltpu.VMEM((2, depth, width), jnp.bfloat16)],
        compiler_params=pltpu.CompilerParams(vmem_limit_bytes=28 * 1024 * 1024),
    )(place, held, other, wide)


def on_device(spectra):
    windows, _, freqs, channels = spectra.shape
    width = channels // 2
    place = jnp.stack([lax.axis_index(a) for a in ("zl", "core", "y", "x")]).astype(jnp.int32)
    zh = lax.axis_index("zh")
    block = jnp.transpose(spectra, (2, 1, 0, 3)).reshape(freqs, 2 * windows, channels)

    def half_of(b):
        low = jnp.concatenate([b[0, :, :width], b[1, :, :width]], axis=1)
        high = jnp.concatenate([b[0, :, width:], b[1, :, width:]], axis=1)
        return jnp.where(zh == 0, low, high)

    partner = permute(block, lambda zl, core, y, x, zh: (zl, core, y, x, 1 - zh))
    pieces = jnp.stack([half_of(block), half_of(partner)])
    near = gather_plane(block)
    held = jnp.stack([to_column(pieces, c, False) for c in range(2)])
    partner, near = lax.optimization_barrier((partner, near))
    wide = whiten_sources(place, [near, gather_plane(partner)])
    held = jnp.concatenate([held] + [along_column(held, d) for d in (1, 2, 3)])
    other = permute(held, lambda zl, core, y, x, zh: (zl, 1 - core, y, x, zh))

    crossed = multiply(place, held, other, wide)
    return jnp.transpose(crossed, (3, 0, 1, 2))


def solution(mesh):
    fine = Mesh(mesh.devices.reshape(tuple(SIZES.values())), AXES)
    return jax.shard_map(
        on_device,
        mesh=fine,
        in_specs=(P(("y", "x", "zh"), None, None, ("zl", "core")),),
        out_specs=P(("zl", "core"), None, None, ("y", "x", "zh")),
        check_vma=False,
    )
```

```python
import functools
import math

import jax
import jax.numpy as jnp
from jax import lax
from jax.experimental import pallas as pl
from jax.experimental.pallas import tpu as pltpu
from jax.sharding import Mesh, PartitionSpec as P

water_factor = 0.5
tiny_eps = 1e-06

SIZES = dict(zl=8, core=2, y=4, x=4, zh=2)
AXES = tuple(SIZES)


def coordinates():
    out = [()]
    for size in SIZES.values():
        out = [c + (i,) for c in out for i in range(size)]
    return out


def number(c):
    n = 0
    for i, size in zip(c, SIZES.values()):
        n = n * size + i % size
    return n


def permute(value, target):
    pairs = [(number(c), number(target(*c))) for c in coordinates()]
    return lax.ppermute(value, AXES, pairs)


def gather_plane(block):
    copies = jnp.broadcast_to(block, (16,) + block.shape)
    return lax.all_to_all(copies, ("y", "x"), 0, 0)


def to_column(value, copy, cross):
    def target(zl, core, y, x, zh):
        s, g = zl * 2 + core, y * 4 + x
        group, slot = ((g ^ s) + copy) % 2, (g ^ s) // 2
        return (group * 4 + slot // 2, slot % 2, s // 4, s % 4, 1 - zh if cross else zh)

    return permute(value, target)


def along_column(value, distance):
    return permute(value, lambda zl, core, y, x, zh: (zl ^ distance, core, y, x, zh))


def energy_of(block):
    values = block.astype(jnp.float32)
    half = values.shape[0] // 2
    real, imag = values[:half], values[half:]
    return real, imag, real * real + imag * imag


def fold(energy):
    return energy.reshape(energy.shape[0] // 8, 8, energy.shape[1]).sum(axis=0)


def floor_of(total, windows):
    return (water_factor / windows) * jnp.sum(total, axis=0, keepdims=True) + tiny_eps


def stacked(upper, lower):
    return jnp.concatenate([upper, lower], axis=0).astype(jnp.bfloat16)


def energy_kernel(blocks, out):
    freqs, rows, channels = blocks.shape[1:]
    for f in range(freqs):

        def add(a, total):
            for i in range(4):
                total = total + fold(energy_of(blocks[a * 4 + i, f])[2])
            return total

        out[f] = lax.fori_loop(0, 4, add, jnp.zeros((8, channels), jnp.float32))


def whiten_kernel(near, far, energies, wide):
    sources = (near, far)
    freqs, rows, channels = sources[0].shape[1:]
    windows = 16 * rows
    for f in range(freqs):

        def add(a, total):
            for i in range(4):
                total = total + fold(energy_of(far[a * 4 + i, f])[2])
            return total

        floor = floor_of(lax.fori_loop(0, 4, add, energies[f]), windows)

        def whiten(a, carry):
            for i in range(4):
                for zr, ref in enumerate(sources):
                    real, imag, energy = energy_of(ref[a * 4 + i, f])
                    scale = lax.rsqrt(energy + floor)
                    real, imag = real * scale, imag * scale
                    row = pl.multiple_of((zr * 16 + a * 4 + i) * rows, rows)
                    wide[f, pl.ds(row, rows), :channels] = stacked(real, imag)
                    wide[f, pl.ds(row, rows), channels:] = stacked(imag, -real)
            return carry

        lax.fori_loop(0, 4, whiten, 0)


def multiply_kernel(place, held, other, wide, out, left, products, sems):
    zl, core, column = place[0], place[1], place[2] * 4 + place[3]
    rows, channels = held.shape[2:]
    width = channels // 2
    windows = 16 * rows

    def add(a, total):
        for ref in (held, other):
            for zr in range(2):
                total = total + fold(energy_of(ref[a, zr])[2])
        return total

    floor = floor_of(lax.fori_loop(0, 8, add, jnp.zeros((8, channels), jnp.float32)), windows)

    def whiten(a, carry):
        along = lax.rem(lax.bitwise_xor(zl, a // 2), 4)
        copy = lax.rem(zl // 4 + a, 2)
        for n, ref in enumerate((held, other)):
            g = lax.bitwise_xor(along * 4 + lax.bitwise_xor(core, n) * 2 + copy, column)
            for zr in range(2):
                real, imag, energy = energy_of(ref[a, zr])
                scale = lax.rsqrt(energy + floor)
                row = pl.multiple_of((zr * 16 + g) * rows, rows)
                block = stacked(real * scale, imag * scale)
                for f in range(2):
                    left[f, pl.ds(row, rows), :] = block[:, f * width : (f + 1) * width]
        return carry

    lax.fori_loop(0, 8, whiten, 0)

    stack_scale = 1.0 / math.sqrt(windows)
    copies = []
    for f in range(2):
        product = lax.dot_general(left[f], wide[f], (((0,), (0,)), ((), ())), preferred_element_type=jnp.float32)
        product = product * stack_scale
        for part in range(2):
            products[part, f] = product[:, part * channels : (part + 1) * channels]
            copy = pltpu.make_async_copy(products.at[part, f], out.at[part, f], sems.at[part, f])
            copy.start()
            copies.append(copy)
    for copy in copies:
        copy.wait()


VMEM = pl.BlockSpec(memory_space=pltpu.VMEM)
SMEM = pl.BlockSpec(memory_space=pltpu.SMEM)


def energies_of(blocks):
    freqs, rows, channels = blocks.shape[1:]
    return pl.pallas_call(
        energy_kernel,
        out_shape=jax.ShapeDtypeStruct((freqs, 8, channels), jnp.float32),
        in_specs=[VMEM],
        out_specs=VMEM,
        compiler_params=pltpu.CompilerParams(vmem_limit_bytes=8 * 1024 * 1024),
    )(blocks)


def whiten_sources(near, far, energies):
    freqs, rows, channels = near.shape[1:]
    depth = 32 * rows
    return pl.pallas_call(
        whiten_kernel,
        out_shape=jax.ShapeDtypeStruct((freqs, depth, 2 * channels), jnp.bfloat16),
        in_specs=[VMEM] * 3,
        out_specs=VMEM,
        compiler_params=pltpu.CompilerParams(vmem_limit_bytes=20 * 1024 * 1024),
    )(near, far, energies)


def multiply(place, held, other, wide):
    rows, channels = held.shape[2:]
    depth, width = 32 * rows, channels // 2
    return pl.pallas_call(
        multiply_kernel,
        out_shape=jax.ShapeDtypeStruct((2, 2, width, channels), jnp.float32),
        in_specs=[SMEM, VMEM, VMEM, VMEM],
        out_specs=pl.BlockSpec(memory_space=pl.ANY),
        scratch_shapes=[
            pltpu.VMEM((2, depth, width), jnp.bfloat16),
            pltpu.VMEM((2, 2, width, channels), jnp.float32),
            pltpu.SemaphoreType.DMA((2, 2)),
        ],
        compiler_params=pltpu.CompilerParams(vmem_limit_bytes=20 * 1024 * 1024),
    )(place, held, other, wide)


def on_device(spectra):
    windows, _, freqs, channels = spectra.shape
    width = channels // 2
    place = jnp.stack([lax.axis_index(a) for a in ("zl", "core", "y", "x")]).astype(jnp.int32)
    zh = lax.axis_index("zh")
    block = jnp.transpose(spectra, (2, 1, 0, 3)).reshape(freqs, 2 * windows, channels)

    def half_of(b):
        low = jnp.concatenate([b[0, :, :width], b[1, :, :width]], axis=1)
        high = jnp.concatenate([b[0, :, width:], b[1, :, width:]], axis=1)
        return jnp.where(zh == 0, low, high)

    partner = permute(block, lambda zl, core, y, x, zh: (zl, core, y, x, 1 - zh))
    pieces = jnp.stack([half_of(block), half_of(partner)])
    near = gather_plane(block)
    held = jnp.stack([to_column(pieces, c, False) for c in range(2)])
    partner, near = lax.optimization_barrier((partner, near))
    wide = whiten_sources(near, gather_plane(partner), energies_of(near))
    held = jnp.concatenate([held] + [along_column(held, d) for d in (1, 2, 3)])
    other = permute(held, lambda zl, core, y, x, zh: (zl, 1 - core, y, x, zh))

    crossed = multiply(place, held, other, wide)
    return jnp.transpose(crossed, (3, 0, 1, 2))


def solution(mesh):
    fine = Mesh(mesh.devices.reshape(tuple(SIZES.values())), AXES)
    return jax.shard_map(
        on_device,
        mesh=fine,
        in_specs=(P(("y", "x", "zh"), None, None, ("zl", "core")),),
        out_specs=P(("zl", "core"), None, None, ("y", "x", "zh")),
        check_vma=False,
    )
```

```python
import functools
import math

import jax
import jax.numpy as jnp
from jax import lax
from jax.experimental import pallas as pl
from jax.experimental.pallas import tpu as pltpu
from jax.sharding import Mesh, PartitionSpec as P

water_factor = 0.5
tiny_eps = 1e-06

SIZES = dict(zl=8, core=2, y=4, x=4, zh=2)
AXES = tuple(SIZES)


def coordinates():
    out = [()]
    for size in SIZES.values():
        out = [c + (i,) for c in out for i in range(size)]
    return out


def number(c):
    n = 0
    for i, size in zip(c, SIZES.values()):
        n = n * size + i % size
    return n


def permute(value, target):
    pairs = [(number(c), number(target(*c))) for c in coordinates()]
    return lax.ppermute(value, AXES, pairs)


def gather_plane(block):
    copies = jnp.broadcast_to(block, (16,) + block.shape)
    return lax.all_to_all(copies, ("y", "x"), 0, 0)


def to_column(value, copy, cross):
    def target(zl, core, y, x, zh):
        s, g = zl * 2 + core, y * 4 + x
        group, slot = ((g ^ s) + copy) % 2, (g ^ s) // 2
        return (group * 4 + slot // 2, slot % 2, s // 4, s % 4, 1 - zh if cross else zh)

    return permute(value, target)


def along_column(value, distance):
    return permute(value, lambda zl, core, y, x, zh: (zl ^ distance, core, y, x, zh))


def energy_of(block):
    values = block.astype(jnp.float32)
    half = values.shape[0] // 2
    real, imag = values[:half], values[half:]
    return real, imag, real * real + imag * imag


def fold(energy):
    return energy.reshape(energy.shape[0] // 8, 8, energy.shape[1]).sum(axis=0)


def floor_of(total, windows):
    return (water_factor / windows) * jnp.sum(total, axis=0, keepdims=True) + tiny_eps


def stacked(upper, lower):
    return jnp.concatenate([upper, lower], axis=0).astype(jnp.bfloat16)


def energy_kernel(blocks, out):
    freqs, rows, channels = blocks.shape[1:]
    for f in range(freqs):

        def add(a, total):
            for i in range(4):
                total = total + fold(energy_of(blocks[a * 4 + i, f])[2])
            return total

        out[f] = lax.fori_loop(0, 4, add, jnp.zeros((8, channels), jnp.float32))


def whiten_kernel(near, arrived, energies, wide, far, sems):
    sources = (near, far)
    freqs, rows, channels = sources[0].shape[1:]
    windows = 16 * rows
    copies = [
        pltpu.make_async_copy(arrived.at[pl.ds(4 * n, 4)], far.at[pl.ds(4 * n, 4)], sems.at[n]) for n in range(4)
    ]
    for copy in copies:
        copy.start()
    totals = [energies[f] for f in range(freqs)]
    for n, copy in enumerate(copies):
        copy.wait()
        for f in range(freqs):
            for i in range(4):
                totals[f] = totals[f] + fold(energy_of(far[4 * n + i, f])[2])
    for f in range(freqs):
        floor = floor_of(totals[f], windows)

        def whiten(a, carry):
            for i in range(4):
                for zr, ref in enumerate(sources):
                    real, imag, energy = energy_of(ref[a * 4 + i, f])
                    scale = lax.rsqrt(energy + floor)
                    real, imag = real * scale, imag * scale
                    row = pl.multiple_of((zr * 16 + a * 4 + i) * rows, rows)
                    wide[f, pl.ds(row, rows), :channels] = stacked(real, imag)
                    wide[f, pl.ds(row, rows), channels:] = stacked(imag, -real)
            return carry

        lax.fori_loop(0, 4, whiten, 0)


def multiply_kernel(place, held, arrived, wide, out, other, left, products, sems, other_sem):
    zl, core, column = place[0], place[1], place[2] * 4 + place[3]
    rows, channels = held.shape[2:]
    width = channels // 2
    windows = 16 * rows

    fetch = pltpu.make_async_copy(arrived, other, other_sem)
    fetch.start()

    def energies_in(ref, total):
        def add(a, total):
            for zr in range(2):
                total = total + fold(energy_of(ref[a, zr])[2])
            return total

        return lax.fori_loop(0, 8, add, total)

    total = energies_in(held, jnp.zeros((8, channels), jnp.float32))
    fetch.wait()
    floor = floor_of(energies_in(other, total), windows)

    def whiten(a, carry):
        along = lax.rem(lax.bitwise_xor(zl, a // 2), 4)
        copy = lax.rem(zl // 4 + a, 2)
        for n, ref in enumerate((held, other)):
            g = lax.bitwise_xor(along * 4 + lax.bitwise_xor(core, n) * 2 + copy, column)
            for zr in range(2):
                real, imag, energy = energy_of(ref[a, zr])
                scale = lax.rsqrt(energy + floor)
                row = pl.multiple_of((zr * 16 + g) * rows, rows)
                block = stacked(real * scale, imag * scale)
                for f in range(2):
                    left[f, pl.ds(row, rows), :] = block[:, f * width : (f + 1) * width]
        return carry

    lax.fori_loop(0, 8, whiten, 0)

    stack_scale = 1.0 / math.sqrt(windows)
    copies = []
    for f in range(2):
        product = lax.dot_general(left[f], wide[f], (((0,), (0,)), ((), ())), preferred_element_type=jnp.float32)
        product = product * stack_scale
        for part in range(2):
            products[part, f] = product[:, part * channels : (part + 1) * channels]
            copy = pltpu.make_async_copy(products.at[part, f], out.at[part, f], sems.at[part, f])
            copy.start()
            copies.append(copy)
    for copy in copies:
        copy.wait()


VMEM = pl.BlockSpec(memory_space=pltpu.VMEM)
SMEM = pl.BlockSpec(memory_space=pltpu.SMEM)


def energies_of(blocks):
    freqs, rows, channels = blocks.shape[1:]
    return pl.pallas_call(
        energy_kernel,
        out_shape=jax.ShapeDtypeStruct((freqs, 8, channels), jnp.float32),
        in_specs=[VMEM],
        out_specs=VMEM,
        compiler_params=pltpu.CompilerParams(vmem_limit_bytes=8 * 1024 * 1024),
    )(blocks)


def whiten_sources(near, far, energies):
    freqs, rows, channels = near.shape[1:]
    depth = 32 * rows
    return pl.pallas_call(
        whiten_kernel,
        out_shape=jax.ShapeDtypeStruct((freqs, depth, 2 * channels), jnp.bfloat16),
        in_specs=[VMEM, pl.BlockSpec(memory_space=pl.ANY), VMEM],
        out_specs=VMEM,
        scratch_shapes=[pltpu.VMEM(far.shape, far.dtype), pltpu.SemaphoreType.DMA((4,))],
        compiler_params=pltpu.CompilerParams(vmem_limit_bytes=20 * 1024 * 1024),
    )(near, far, energies)


def multiply(place, held, other, wide):
    rows, channels = held.shape[2:]
    depth, width = 32 * rows, channels // 2
    return pl.pallas_call(
        multiply_kernel,
        out_shape=jax.ShapeDtypeStruct((2, 2, width, channels), jnp.float32),
        in_specs=[SMEM, VMEM, pl.BlockSpec(memory_space=pl.ANY), VMEM],
        out_specs=pl.BlockSpec(memory_space=pl.ANY),
        scratch_shapes=[
            pltpu.VMEM(other.shape, other.dtype),
            pltpu.VMEM((2, depth, width), jnp.bfloat16),
            pltpu.VMEM((2, 2, width, channels), jnp.float32),
            pltpu.SemaphoreType.DMA((2, 2)),
            pltpu.SemaphoreType.DMA,
        ],
        compiler_params=pltpu.CompilerParams(vmem_limit_bytes=20 * 1024 * 1024),
    )(place, held, other, wide)


def on_device(spectra):
    windows, _, freqs, channels = spectra.shape
    width = channels // 2
    place = jnp.stack([lax.axis_index(a) for a in ("zl", "core", "y", "x")]).astype(jnp.int32)
    zh = lax.axis_index("zh")
    block = jnp.transpose(spectra, (2, 1, 0, 3)).reshape(freqs, 2 * windows, channels)

    def half_of(b):
        low = jnp.concatenate([b[0, :, :width], b[1, :, :width]], axis=1)
        high = jnp.concatenate([b[0, :, width:], b[1, :, width:]], axis=1)
        return jnp.where(zh == 0, low, high)

    partner = permute(block, lambda zl, core, y, x, zh: (zl, core, y, x, 1 - zh))
    pieces = jnp.stack([half_of(block), half_of(partner)])
    near = gather_plane(block)
    held = jnp.stack([to_column(pieces, c, False) for c in range(2)])
    partner, near = lax.optimization_barrier((partner, near))
    wide = whiten_sources(near, gather_plane(partner), energies_of(near))
    held = jnp.concatenate([held] + [along_column(held, d) for d in (1, 2, 3)])
    other = permute(held, lambda zl, core, y, x, zh: (zl, 1 - core, y, x, zh))

    crossed = multiply(place, held, other, wide)
    return jnp.transpose(crossed, (3, 0, 1, 2))


def solution(mesh):
    fine = Mesh(mesh.devices.reshape(tuple(SIZES.values())), AXES)
    return jax.shard_map(
        on_device,
        mesh=fine,
        in_specs=(P(("y", "x", "zh"), None, None, ("zl", "core")),),
        out_specs=P(("zl", "core"), None, None, ("y", "x", "zh")),
        check_vma=False,
    )
```

```python
import functools
import math

import jax
import jax.numpy as jnp
from jax import lax
from jax.experimental import pallas as pl
from jax.experimental.pallas import tpu as pltpu
from jax.sharding import Mesh, PartitionSpec as P

water_factor = 0.5
tiny_eps = 1e-06

SIZES = dict(zl=8, core=2, y=4, x=4, zh=2)
AXES = tuple(SIZES)


def coordinates():
    out = [()]
    for size in SIZES.values():
        out = [c + (i,) for c in out for i in range(size)]
    return out


def number(c):
    n = 0
    for i, size in zip(c, SIZES.values()):
        n = n * size + i % size
    return n


def permute(value, target):
    pairs = [(number(c), number(target(*c))) for c in coordinates()]
    return lax.ppermute(value, AXES, pairs)


def gather_plane(block):
    copies = jnp.broadcast_to(block, (16,) + block.shape)
    return lax.all_to_all(copies, ("y", "x"), 0, 0)


def to_column(value, copy, cross):
    def target(zl, core, y, x, zh):
        s, g = zl * 2 + core, y * 4 + x
        group, slot = ((g ^ s) + copy) % 2, (g ^ s) // 2
        return (group * 4 + slot // 2, slot % 2, s // 4, s % 4, 1 - zh if cross else zh)

    return permute(value, target)


def along_column(value, distance):
    return permute(value, lambda zl, core, y, x, zh: (zl ^ distance, core, y, x, zh))


def energy_of(block):
    values = block.astype(jnp.float32)
    half = values.shape[0] // 2
    real, imag = values[:half], values[half:]
    return real, imag, real * real + imag * imag


def fold(energy):
    return energy.reshape(energy.shape[0] // 8, 8, energy.shape[1]).sum(axis=0)


def floor_of(total, windows):
    return (water_factor / windows) * jnp.sum(total, axis=0, keepdims=True) + tiny_eps


def stacked(upper, lower):
    return jnp.concatenate([upper, lower], axis=0).astype(jnp.bfloat16)


def energy_kernel(blocks, out):
    freqs, rows, channels = blocks.shape[1:]
    for f in range(freqs):

        def add(a, total):
            for i in range(4):
                total = total + fold(energy_of(blocks[a * 4 + i, f])[2])
            return total

        out[f] = lax.fori_loop(0, 4, add, jnp.zeros((8, channels), jnp.float32))


def whiten_kernel(near, arrived, energies, wide, far, sems):
    sources = (near, far)
    freqs, rows, channels = sources[0].shape[1:]
    windows = 16 * rows
    copies = [
        pltpu.make_async_copy(arrived.at[pl.ds(4 * n, 4)], far.at[pl.ds(4 * n, 4)], sems.at[n]) for n in range(4)
    ]
    for copy in copies:
        copy.start()
    totals = [energies[f] for f in range(freqs)]
    for n, copy in enumerate(copies):
        copy.wait()
        for f in range(freqs):
            for i in range(4):
                totals[f] = totals[f] + fold(energy_of(far[4 * n + i, f])[2])
    for f in range(freqs):
        floor = floor_of(totals[f], windows)

        def whiten(a, carry):
            for i in range(4):
                for zr, ref in enumerate(sources):
                    real, imag, energy = energy_of(ref[a * 4 + i, f])
                    scale = lax.rsqrt(energy + floor)
                    real, imag = real * scale, imag * scale
                    row = pl.multiple_of((zr * 16 + a * 4 + i) * rows, rows)
                    wide[f, pl.ds(row, rows), :channels] = stacked(real, imag)
                    wide[f, pl.ds(row, rows), channels:] = stacked(imag, -real)
            return carry

        lax.fori_loop(0, 4, whiten, 0)


def multiply_kernel(place, held, other, wide, out, left, products, sems):
    zl, core, column = place[0], place[1], place[2] * 4 + place[3]
    rows, channels = held.shape[2:]
    width = channels // 2
    windows = 16 * rows

    def add(a, total):
        for ref in (held, other):
            for zr in range(2):
                total = total + fold(energy_of(ref[a, zr])[2])
        return total

    floor = floor_of(lax.fori_loop(0, 8, add, jnp.zeros((8, channels), jnp.float32)), windows)

    def whiten(a, carry):
        along = lax.rem(lax.bitwise_xor(zl, a // 2), 4)
        copy = lax.rem(zl // 4 + a, 2)
        for n, ref in enumerate((held, other)):
            g = lax.bitwise_xor(along * 4 + lax.bitwise_xor(core, n) * 2 + copy, column)
            for zr in range(2):
                real, imag, energy = energy_of(ref[a, zr])
                scale = lax.rsqrt(energy + floor)
                row = pl.multiple_of((zr * 16 + g) * rows, rows)
                block = stacked(real * scale, imag * scale)
                for f in range(2):
                    left[f, pl.ds(row, rows), :] = block[:, f * width : (f + 1) * width]
        return carry

    lax.fori_loop(0, 8, whiten, 0)

    stack_scale = 1.0 / math.sqrt(windows)
    copies = []
    for f in range(2):
        product = lax.dot_general(left[f], wide[f], (((0,), (0,)), ((), ())), preferred_element_type=jnp.float32)
        product = product * stack_scale
        for part in range(2):
            products[part, f] = product[:, part * channels : (part + 1) * channels]
            copy = pltpu.make_async_copy(products.at[part, f], out.at[part, f], sems.at[part, f])
            copy.start()
            copies.append(copy)
    for copy in copies:
        copy.wait()


VMEM = pl.BlockSpec(memory_space=pltpu.VMEM)
SMEM = pl.BlockSpec(memory_space=pltpu.SMEM)


def energies_of(blocks):
    freqs, rows, channels = blocks.shape[1:]
    return pl.pallas_call(
        energy_kernel,
        out_shape=jax.ShapeDtypeStruct((freqs, 8, channels), jnp.float32),
        in_specs=[VMEM],
        out_specs=VMEM,
        compiler_params=pltpu.CompilerParams(vmem_limit_bytes=8 * 1024 * 1024),
    )(blocks)


def whiten_sources(near, far, energies):
    freqs, rows, channels = near.shape[1:]
    depth = 32 * rows
    return pl.pallas_call(
        whiten_kernel,
        out_shape=jax.ShapeDtypeStruct((freqs, depth, 2 * channels), jnp.bfloat16),
        in_specs=[VMEM, pl.BlockSpec(memory_space=pl.ANY), VMEM],
        out_specs=VMEM,
        scratch_shapes=[pltpu.VMEM(far.shape, far.dtype), pltpu.SemaphoreType.DMA((4,))],
        compiler_params=pltpu.CompilerParams(vmem_limit_bytes=20 * 1024 * 1024),
    )(near, far, energies)


def multiply(place, held, other, wide):
    rows, channels = held.shape[2:]
    depth, width = 32 * rows, channels // 2
    return pl.pallas_call(
        multiply_kernel,
        out_shape=jax.ShapeDtypeStruct((2, 2, width, channels), jnp.float32),
        in_specs=[SMEM, VMEM, VMEM, VMEM],
        out_specs=pl.BlockSpec(memory_space=pl.ANY),
        scratch_shapes=[
            pltpu.VMEM((2, depth, width), jnp.bfloat16),
            pltpu.VMEM((2, 2, width, channels), jnp.float32),
            pltpu.SemaphoreType.DMA((2, 2)),
        ],
        compiler_params=pltpu.CompilerParams(vmem_limit_bytes=20 * 1024 * 1024),
    )(place, held, other, wide)


def on_device(spectra):
    windows, _, freqs, channels = spectra.shape
    width = channels // 2
    place = jnp.stack([lax.axis_index(a) for a in ("zl", "core", "y", "x")]).astype(jnp.int32)
    zh = lax.axis_index("zh")
    block = jnp.transpose(spectra, (2, 1, 0, 3)).reshape(freqs, 2 * windows, channels)

    def half_of(b):
        low = jnp.concatenate([b[0, :, :width], b[1, :, :width]], axis=1)
        high = jnp.concatenate([b[0, :, width:], b[1, :, width:]], axis=1)
        return jnp.where(zh == 0, low, high)

    partner = permute(block, lambda zl, core, y, x, zh: (zl, core, y, x, 1 - zh))
    pieces = jnp.stack([half_of(block), half_of(partner)])
    near = gather_plane(block)
    held = jnp.stack([to_column(pieces, c, False) for c in range(2)])
    partner, near = lax.optimization_barrier((partner, near))
    wide = whiten_sources(near, gather_plane(partner), energies_of(near))
    held = jnp.concatenate([held] + [along_column(held, d) for d in (1, 2, 3)])
    other = permute(held, lambda zl, core, y, x, zh: (zl, 1 - core, y, x, zh))

    crossed = multiply(place, held, other, wide)
    return jnp.transpose(crossed, (3, 0, 1, 2))


def solution(mesh):
    fine = Mesh(mesh.devices.reshape(tuple(SIZES.values())), AXES)
    return jax.shard_map(
        on_device,
        mesh=fine,
        in_specs=(P(("y", "x", "zh"), None, None, ("zl", "core")),),
        out_specs=P(("zl", "core"), None, None, ("y", "x", "zh")),
        check_vma=False,
    )
```
